32 devices in a mesh: parts: 2 (over y), rep: 4 (over x, core), tp: 4 (over z).
Axes of the slice: x: 2, y: 2, z: 4, core: 2. Of those that a mesh axis runs over, the one named last changes fastest.
Arguments:
- gate_inputs: bfloat16 [6, 128, 8192], P(None, ('parts', 'rep'), 'tp'), parts along dimension 1, may hold values from -12 to 12
- conv_inputs: bfloat16 [6, 128, 8192], P(None, ('parts', 'rep'), 'tp'), parts along dimension 1, may hold values from -6 to 6
- bc_inputs: bfloat16 [6, 128, 2048], P(None, ('parts', 'rep')), parts along dimension 1, may hold values from -6 to 6
- delta_inputs: bfloat16 [6, 128, 128], P(None, ('parts', 'rep'), 'tp'), parts along dimension 1, may hold values from -5 to 5
- conv_weight: float32 [4, 8192], P(None, 'tp'), may hold values from -3 to 3
- conv_bias: float32 [8192], P('tp'), may hold values from -3 to 3
- bc_weight: float32 [4, 2048], replicated, may hold values from -3 to 3
- bc_bias: float32 [2048], replicated, may hold values from -3 to 3
- delta_bias: float32 [128], P('tp'), may hold values from -2 to 0.5
- decay_rate: float32 [128], P('tp'), may hold values from 0.02 to 3
- skip_gain: float32 [128], P('tp'), may hold values from 1 to 4
- norm_gain: float32 [8192], P('tp'), may hold values from 0.1 to 1.9
- out_weight: bfloat16 [8192, 4096], P('tp'), may hold values from -0.09375 to 0.09375
- ssd_state: float32 [128, 128, 64, 128], P(('parts', 'rep'), 'tp'), parts along dimension 0, may hold values from -3 to 3
- conv_state: bfloat16 [128, 3, 8192], P(('parts', 'rep'), None, 'tp'), parts along dimension 0, may hold values from -6 to 6
- bc_state: bfloat16 [128, 3, 2048], P(('parts', 'rep')), parts along dimension 0, may hold values from -6 to 6
- finish_step: int32 [128], P(('parts', 'rep')), parts along dimension 0, may hold values from 1 to 12, as said below
- move_plan: int32 [2, 4, 4, 2, 2], P('parts'), parts along dimension 0, may hold values from -1 to 15, as said below
Outputs:
- layer_out: bfloat16 [6, 128, 4096], P(None, ('parts', 'rep'), 'tp'), parts along dimension 1
The draws below stay inside these ranges and needn't reach their ends.
There are 2 independent parts, one for each index of `parts`. The reference program is written for one: setup_inputs(seed, part) draws one part's arguments, and reference() takes and returns one part's arrays. A program takes and returns all parts, laid end to end along the dimension named above; an argument that names none is the same for every part. Nothing has to cross between parts.
Inputs may be any that keep to these rules, and one draw needn't show every extreme that they name: A slot emits outputs at steps t < finish_step. `move_plan`: entry [k, i, j, c] is (source slot on replica i, destination slot on replica j) or (-1, -1) when unused; no entry has i == j; within one k, the used source slots of one replica are distinct and the used destination slots of one replica are distinct; at every migration some pair (i, j) uses all 2 lanes and some replica receives 2 rollouts from every other replica.
All inputs are finite; a program needn't handle non-finite values.
Results may differ from the reference program's by a relative error of at most 0.005.
Values may be sent and summed in bfloat16 or wider, within the bound.
A program may use at most 192 MiB of HBM per device.

```python
import math
import jax
import jax.numpy as jnp
from jax import lax

D = 4096
HEADS = 128
HEAD_DIM = 64
STATE = 128
GROUPS = 8
KERNEL = 4
SLOTS = 16
STEPS = 6
PERIOD = 3
CAP = 2
MIGR = 1
ROLLOUTS = 64
INNER = 8192
BC_WIDTH = 2048
N_REP = 4


def life_table(key):
    table_key = jax.random.fold_in(key, 17)
    replica_ids = jnp.arange(ROLLOUTS, dtype=jnp.int32) // SLOTS
    spans = STEPS // 2 + replica_ids * 3 * STEPS // (2 * max(N_REP - 1, 1))
    raw_bits = jax.random.randint(table_key, (ROLLOUTS,), 0, 1 << 20)
    life_ends = 1 + raw_bits % spans
    life_ends = life_ends.at[0].set(1).at[ROLLOUTS - 1].set(2 * STEPS)
    return life_ends.astype(jnp.int32)


def draw_finish_step(key, part):
    return life_table(key)


def draw_move_plan(key, part):
    life_ends = life_table(key)
    plan_key = jax.random.fold_in(key, 29)
    width = (N_REP - 1) * CAP
    rep_ids = jnp.arange(N_REP, dtype=jnp.int32)
    lane_ids = jnp.arange(CAP, dtype=jnp.int32)
    slot_ids = jnp.arange(SLOTS, dtype=jnp.int32)
    sender = jnp.broadcast_to(rep_ids[:, None, None], (N_REP, N_REP, CAP))
    receiver = jnp.broadcast_to(rep_ids[None, :, None], (N_REP, N_REP, CAP))
    lanes = jnp.broadcast_to(lane_ids[None, None, :], (N_REP, N_REP, CAP))
    layers = []
    for move_index in range(MIGR):
        moment = (move_index + 1) * PERIOD
        round_key = jax.random.fold_in(plan_key, move_index)
        key_a, key_b, key_c, key_d = jax.random.split(round_key, 4)
        is_live = (life_ends > moment).astype(jnp.int32).reshape(N_REP, SLOTS)
        noise_a = jax.random.randint(key_a, (N_REP, SLOTS), 0, 1 << 14) * SLOTS + slot_ids[None, :]
        noise_b = jax.random.randint(key_b, (N_REP, SLOTS), 0, 1 << 14) * SLOTS + slot_ids[None, :]
        source_order = lax.top_k(is_live * (1 << 24) + noise_a, width)[1].astype(jnp.int32)
        target_order = lax.top_k((1 - is_live) * (1 << 24) + noise_b, width)[1].astype(jnp.int32)
        out_pos = jnp.minimum((receiver - sender - 1) % N_REP * CAP + lanes, width - 1)
        in_pos = jnp.minimum((sender - receiver - 1) % N_REP * CAP + lanes, width - 1)
        source_slot = source_order[sender, out_pos]
        target_slot = target_order[receiver, in_pos]
        full_target = jax.random.randint(key_d, (), 0, N_REP)
        coin_flip = jax.random.randint(key_c, (N_REP, N_REP, CAP), 0, 2)
        is_used = (sender != receiver) & ((lanes == 0) | (receiver == (sender + 1) % N_REP) | (receiver == full_target) | (coin_flip == 1))
        source_slot = jnp.where(is_used, source_slot, -1)
        target_slot = jnp.where(is_used, target_slot, -1)
        layers.append(jnp.stack([source_slot, target_slot], -1))
        from_rows = jnp.where(is_used, source_slot + sender * SLOTS, ROLLOUTS).reshape(-1)
        to_rows = jnp.where(is_used, target_slot + receiver * SLOTS, ROLLOUTS).reshape(-1)
        fetch_rows = jnp.minimum(from_rows, ROLLOUTS - 1)
        moved_ends = life_ends[fetch_rows]
        life_ends = life_ends.at[from_rows].set(0, mode='drop').at[to_rows].set(moved_ends, mode='drop')
    return jnp.stack(layers, 0).astype(jnp.int32)


def draw_gate_inputs(key, part):
    key = jax.random.fold_in(key, 3)
    channel = jnp.arange(INNER, dtype=jnp.float32) / max(INNER - 1, 1)
    factor = jnp.exp(jnp.log(3.0) * channel)
    values = jnp.clip(jax.random.normal(key, (STEPS, ROLLOUTS, INNER), jnp.float32), -4.0, 4.0) * factor
    return values.astype(jnp.bfloat16)


def strengthened(result, rng, source, target, blocks, factor):
    def block_of(axis_at):
        return (jnp.arange(result.shape[axis_at]) // (result.shape[axis_at] // blocks)).reshape((-1,) + (1,) * (result.ndim - 1 - axis_at))

    near = jax.random.permutation(rng, blocks)[block_of(target)]
    other_side = (block_of(target) + blocks // 2) % blocks
    return jnp.where((block_of(source) == near) | (block_of(source) == other_side), factor * result, result)


def shard_levels(key, shape, shards, least, largest):
    factor_of, own = 1.0, jax.random.fold_in(key, 6)
    for dim, parts in shards:
        heights = jnp.exp(jax.random.uniform(jax.random.fold_in(own, dim), (parts,), jnp.float32, least / len(shards), largest / len(shards)))
        factor_of = factor_of * jnp.repeat(heights, shape[dim] // parts).reshape([-1 if axis == dim else 1 for axis in range(len(shape))])
    return factor_of


def scatter_about(stream_key, dims, spread, most, shards=(), kind=jnp.bfloat16):
    entries = jax.random.normal(stream_key, dims, jnp.float32) * spread
    if len(shards) > 0:
        entries = shard_levels(stream_key, dims, shards, -0.22, 0.18) * entries
    return jnp.clip(entries, min=-most, max=most).astype(kind)


def gaussian_with(key, shape, deviation, bound, pieces, heavy, kind=jnp.bfloat16):
    entries = deviation * jax.random.normal(key, shape, jnp.float32)
    if pieces:
        entries = entries * shard_levels(key, shape, pieces, -0.22, 0.18)
    return jnp.clip(strengthened(entries, jax.random.fold_in(key, 3), *heavy), -bound, bound).astype(kind)


def setup_inputs(seed: int = 0, part: int = 0) -> dict:
    seeds = jax.random.split(jax.random.key(seed), 19)
    part_keys = jax.random.split(jax.random.fold_in(seeds[18], part), 19)
    gate_inputs = draw_gate_inputs(jax.random.fold_in(jax.random.fold_in(seeds[18], part), 71), part)
    conv_inputs = scatter_about(part_keys[1], (STEPS, ROLLOUTS, INNER), 1.0, 6.0, ((1, 4), (2, 4)))
    bc_inputs = scatter_about(part_keys[2], (STEPS, ROLLOUTS, BC_WIDTH), 1.0, 6.0, ((1, 4),))
    delta_inputs = scatter_about(part_keys[3], (STEPS, ROLLOUTS, HEADS), 1.0, 5.0, ((1, 4), (2, 4)))
    conv_weight = scatter_about(seeds[4], (KERNEL, INNER), KERNEL ** -0.5, 3.0, ((1, 4),), jnp.float32)
    conv_bias = scatter_about(seeds[5], (INNER,), 0.5, 3.0, ((0, 4),), jnp.float32)
    bc_weight = scatter_about(seeds[6], (KERNEL, BC_WIDTH), KERNEL ** -0.5, 3.0, (), jnp.float32)
    bc_bias = scatter_about(seeds[7], (BC_WIDTH,), 0.5, 3.0, (), jnp.float32)
    delta_bias = jnp.clip(-2.0 + 2.5 * jax.random.uniform(seeds[8], (HEADS,), jnp.float32) ** shard_levels(seeds[8], (HEADS,), ((0, 4),), -0.2, 0.2), -2.0, 0.5)
    decay_rate = jnp.clip(jnp.exp(math.log(3.0) - 5.0106353 * jax.random.uniform(seeds[9], (HEADS,), jnp.float32) ** shard_levels(seeds[9], (HEADS,), ((0, 4),), -0.2, 0.2)), 0.02, 3.0)
    skip_gain = jnp.clip(1.0 + 3.0 * jax.random.uniform(seeds[10], (HEADS,), jnp.float32) ** shard_levels(seeds[10], (HEADS,), ((0, 4),), -0.2, 0.2), 1.0, 4.0)
    norm_gain = jnp.clip(1.0 + 0.18 * jax.random.normal(seeds[11], (INNER,), jnp.float32), 0.1, 1.9)
    out_weight = gaussian_with(seeds[12], (INNER, D), INNER ** -0.5, 0.09375, ((0, 4),), (0, 1, 4, 2.0))
    ssd_state = scatter_about(part_keys[13], (ROLLOUTS, HEADS, HEAD_DIM, STATE), 0.5, 3.0, ((0, 4), (1, 4)), jnp.float32)
    conv_state = scatter_about(part_keys[14], (ROLLOUTS, KERNEL - 1, INNER), 1.0, 6.0, ((0, 4), (2, 4)))
    bc_state = scatter_about(part_keys[15], (ROLLOUTS, KERNEL - 1, BC_WIDTH), 1.0, 6.0, ((0, 4),))
    finish_step = draw_finish_step(jax.random.fold_in(jax.random.fold_in(seeds[18], part), 71), part)
    move_plan = draw_move_plan(jax.random.fold_in(jax.random.fold_in(seeds[18], part), 71), part)
    return {"gate_inputs": gate_inputs, "conv_inputs": conv_inputs, "bc_inputs": bc_inputs, "delta_inputs": delta_inputs, "conv_weight": conv_weight, "conv_bias": conv_bias, "bc_weight": bc_weight, "bc_bias": bc_bias, "delta_bias": delta_bias, "decay_rate": decay_rate, "skip_gain": skip_gain, "norm_gain": norm_gain, "out_weight": out_weight, "ssd_state": ssd_state, "conv_state": conv_state, "bc_state": bc_state, "finish_step": finish_step, "move_plan": move_plan}


norm_eps = 1e-05

def state_block(blocks):
    states, x_heads, b_vector, c_vector, step_size, retained, is_live = blocks
    updated = retained[:, :, None, None] * states + (step_size[:, :, None] * x_heads)[:, :, :, None] * b_vector[:, :, None, :]
    states = jnp.where(is_live[:, None, None, None], updated, states)
    head_out = jnp.einsum('rhpn,rhn->rhp', states, c_vector, precision=lax.Precision.HIGHEST)
    return (states, head_out)

def relocate(layer_plan, states, windows, bc_windows, life_ends):
    rep_ids = jnp.arange(N_REP, dtype=jnp.int32)
    sources = layer_plan[..., 0]
    targets = layer_plan[..., 1]
    from_rows = jnp.where(sources >= 0, sources + rep_ids[:, None, None] * SLOTS, ROLLOUTS).reshape(-1).astype(jnp.int32)
    to_rows = jnp.where(targets >= 0, targets + rep_ids[None, :, None] * SLOTS, ROLLOUTS).reshape(-1).astype(jnp.int32)
    fetch_rows = jnp.minimum(from_rows, ROLLOUTS - 1)
    moved_ends = life_ends[fetch_rows]
    life_ends = life_ends.at[from_rows].set(0, mode='drop').at[to_rows].set(moved_ends, mode='drop')
    states = states.at[to_rows].set(states[fetch_rows], mode='drop')
    windows = windows.at[to_rows].set(windows[fetch_rows], mode='drop')
    bc_windows = bc_windows.at[to_rows].set(bc_windows[fetch_rows], mode='drop')
    return (states, windows, bc_windows, life_ends)

def to_blocks(array):
    return array.reshape((N_REP, SLOTS) + array.shape[1:])

def reference(gate_inputs, conv_inputs, bc_inputs, delta_inputs, conv_weight, conv_bias, bc_weight, bc_bias, delta_bias, decay_rate, skip_gain, norm_gain, out_weight, ssd_state, conv_state, bc_state, finish_step, move_plan):
    per_group = HEADS // GROUPS
    states = ssd_state
    windows = conv_state
    bc_windows = bc_state
    life_ends = finish_step
    layer_rows = []
    for step in range(STEPS):
        if step > 0 and step % PERIOD == 0:
            states, windows, bc_windows, life_ends = relocate(move_plan[step // PERIOD - 1], states, windows, bc_windows, life_ends)
        is_live = step < life_ends
        window = jnp.concatenate([windows, conv_inputs[step][:, None, :]], axis=1)
        mixed_conv = lax.optimization_barrier(jnp.sum(window.astype(jnp.float32) * conv_weight[None], axis=1)) + conv_bias
        windows = jnp.where(is_live[:, None, None], window[:, 1:], windows)
        bc_window = jnp.concatenate([bc_windows, bc_inputs[step][:, None, :]], axis=1)
        mixed_bc = lax.optimization_barrier(jnp.sum(bc_window.astype(jnp.float32) * bc_weight[None], axis=1)) + bc_bias
        bc_windows = jnp.where(is_live[:, None, None], bc_window[:, 1:], bc_windows)
        x_heads = jax.nn.silu(mixed_conv).reshape(ROLLOUTS, HEADS, HEAD_DIM)
        bc_act = jax.nn.silu(mixed_bc).reshape(ROLLOUTS, GROUPS, 2, STATE)
        b_vector = jnp.repeat(bc_act[:, :, 0], per_group, axis=1)
        c_vector = jnp.repeat(bc_act[:, :, 1], per_group, axis=1)
        step_size = jax.nn.softplus(delta_inputs[step].astype(jnp.float32) + delta_bias)
        retained = jnp.exp(-step_size * decay_rate)
        blocked = tuple((to_blocks(item) for item in (states, x_heads, b_vector, c_vector, step_size, retained, is_live)))
        states, head_out = lax.map(state_block, blocked)
        states = states.reshape((ROLLOUTS,) + states.shape[2:])
        head_out = head_out.reshape((ROLLOUTS,) + head_out.shape[2:]) + skip_gain[None, :, None] * x_heads
        gated = head_out.reshape(ROLLOUTS, INNER) * jax.nn.silu(gate_inputs[step].astype(jnp.float32))
        inv_rms = lax.rsqrt(lax.optimization_barrier(jnp.mean(gated * gated, axis=1)) + norm_eps)
        hidden = (gated * inv_rms[:, None] * norm_gain).astype(jnp.bfloat16)
        projected = jnp.dot(hidden, out_weight, preferred_element_type=jnp.float32)
        row_scale = is_live.astype(jnp.float32)
        layer_rows.append((projected * row_scale[:, None]).astype(jnp.bfloat16))
    return jnp.stack(layer_rows, 0)
```

```python
import functools

import jax
import jax.numpy as jnp
from jax import lax
from jax.experimental import pallas as pl
from jax.experimental.pallas import tpu as pltpu
from jax.sharding import PartitionSpec as P

HEADS = 128
HEAD_DIM = 64
STATE = 128
GROUPS = 8
PERIOD = 3
CAP = 2
INNER = 8192
EPS = 1e-05
BF16 = jnp.bfloat16
F32 = jnp.float32
MESH = pl.DeviceIdType.MESH


def silu(v):
    return v / (1.0 + jnp.exp(-v))


def softplus(v):
    return jnp.maximum(v, 0.0) + jnp.log1p(jnp.exp(-jnp.abs(v)))


def dot(a, b):
    return lax.dot_general(a, b, (((1,), (0,)), ((), ())), preferred_element_type=F32)


def pack_matrix(slots, moved, peers, pick):
    rows, cols = 16 * peers, moved * slots
    row = lax.broadcasted_iota(jnp.int32, (rows, cols), 0)
    col = lax.broadcasted_iota(jnp.int32, (rows, cols), 1)
    halves = []
    for half in range(2):
        hit = jnp.zeros((rows, cols), F32)
        for o in range(peers):
            for c in range(CAP):
                slot = pick(o, c)
                first = o * 16 + half * CAP * moved + c * moved
                for k in range(moved):
                    match = jnp.where(row == first + k, col, -1) == k * slots + slot
                    valid = jnp.where(slot >= 0, 1.0, 0.0)
                    hit = hit + jnp.where(match, valid, 0.0)
        halves.append(hit.astype(BF16))
    return halves


def unpack_matrix(slots, moved, peers, pick):
    rows, cols = moved * slots, 16 * peers
    row = lax.broadcasted_iota(jnp.int32, (rows, cols), 0)
    col = lax.broadcasted_iota(jnp.int32, (rows, cols), 1)
    halves = []
    for half in range(2):
        hit = jnp.zeros((rows, cols), F32)
        for o in range(peers):
            for c in range(CAP):
                slot = pick(o, c)
                first = o * 16 + half * CAP * moved + c * moved
                for k in range(moved):
                    match = jnp.where(col == first + k, row, -1) == k * slots + slot
                    valid = jnp.where(slot >= 0, 1.0, 0.0)
                    hit = hit + jnp.where(match, valid, 0.0)
        halves.append(hit.astype(BF16))
    return halves


def named(slots, peers, pick):
    row = lax.broadcasted_iota(jnp.int32, (slots, 1), 0)
    hit = jnp.zeros((slots, 1), F32)
    for o in range(peers):
        for c in range(CAP):
            hit = jnp.maximum(hit, jnp.where(row == pick(o, c), 1.0, 0.0))
    return hit


def kernel(
    dims,
    gate_ref,
    conv_ref,
    bc_ref,
    delta_ref,
    conv_w_ref,
    conv_b_ref,
    bc_w_ref,
    bc_b_ref,
    delta_b_ref,
    decay_ref,
    skip_ref,
    gain_ref,
    w_hbm,
    state_hbm,
    conv_state_ref,
    bc_state_ref,
    finish_ref,
    plan_ref,
    out_ref,
    st,
    wv,
    msg,
    got,
    xs,
    bs,
    cs,
    y0,
    gates,
    hidden,
    sq_mine,
    sq_got,
    part,
    part_got,
    rows_out,
    back,
    back_got,
    st_sem,
    w_sem,
    msg_send,
    msg_recv,
    sq_send,
    sq_recv,
    part_send,
    part_recv,
    back_send,
    back_recv,
):
    T, S, IL, HL, NG, R, TP, DL = dims
    GH = HL // NG
    GC = NG * 2 * STATE
    moved = T - PERIOD
    M = moved * S
    me = lax.axis_index("rep")
    tp = lax.axis_index("tp")

    def state_copy(s):
        return pltpu.make_async_copy(state_hbm.at[s], st.at[s], st_sem.at[s])

    def w_copy(o):
        column = pl.multiple_of(lax.rem(tp + o, TP) * DL, DL)
        return pltpu.make_async_copy(w_hbm.at[:, pl.ds(column, DL)], wv.at[o], w_sem.at[o])

    for s in range(S):
        state_copy(s).start()
    for o in list(range(1, TP)) + [0]:
        w_copy(o).start()

    barrier = pltpu.get_barrier_semaphore()
    for o in range(1, R):
        pl.semaphore_signal(
            barrier, inc=1, device_id={"rep": lax.rem(me + o, R)}, device_id_type=MESH
        )
    for o in range(1, TP):
        pl.semaphore_signal(
            barrier, inc=1, device_id={"tp": lax.rem(tp + o, TP)}, device_id_type=MESH
        )

    def entry(source, target, c, which):
        return plan_ref[((source * R + target) * CAP + c) * 2 + which]

    def ahead(o):
        return lax.rem(me + (o + 1), R)

    def behind(o):
        return lax.rem(me + (R - 1 - o), R)

    serve_send = lambda o, c: entry(ahead(o), me, c, 1)
    serve_take = lambda o, c: entry(me, behind(o), c, 0)
    give_send = lambda o, c: entry(me, ahead(o), c, 0)
    give_take = lambda o, c: entry(behind(o), me, c, 1)

    group_column = pl.multiple_of((tp * HL * GROUPS // HEADS) * 2 * STATE, 2 * STATE)
    group_cols = pl.ds(group_column, GC)

    pack_a, pack_b = pack_matrix(S, moved, R - 1, serve_send)
    gate_rows = gate_ref[PERIOD:].reshape(M, IL)
    conv_rows = conv_ref[PERIOD:].reshape(M, IL)
    bc_rows = bc_ref[PERIOD:, :, group_cols].reshape(M, GC)
    delta_rows = delta_ref[PERIOD:].reshape(M, HL)
    packed = dot(pack_a, gate_rows) + dot(pack_b, conv_rows)
    msg[:, :, 0:IL] = packed.astype(BF16).reshape(R - 1, 16, IL)
    msg[:, :, IL : IL + GC] = dot(pack_a, bc_rows).astype(BF16).reshape(R - 1, 16, GC)
    pad_rows = jnp.concatenate([delta_rows.astype(F32), jnp.zeros((M, 128 - HL), F32)], axis=1)
    msg[:, :, IL + GC :] = dot(pack_a, pad_rows.astype(BF16)).astype(BF16).reshape(R - 1, 16, 128)

    pl.semaphore_wait(barrier, R - 1 + TP - 1)

    def msg_copy(o):
        return pltpu.make_async_remote_copy(
            src_ref=msg.at[o],
            dst_ref=got.at[o],
            send_sem=msg_send.at[o],
            recv_sem=msg_recv.at[o],
            device_id={"rep": ahead(o)},
            device_id_type=MESH,
        )

    for o in range(R - 1):
        msg_copy(o).start()

    take_a, take_b = unpack_matrix(S, moved, R - 1, serve_take)
    is_source = named(S, R - 1, serve_take)
    is_target = named(S, R - 1, give_take)
    own = 1.0 - is_source
    own_rows = jnp.concatenate([own] * moved, axis=0)

    conv_old = conv_state_ref[...].astype(F32)
    bc_old = bc_state_ref[:, :, group_cols].astype(F32)

    for o in range(R - 1):
        msg_copy(o).wait()
    arrived = got[...].reshape((R - 1) * 16, IL + GC + 128)
    new_gate = dot(take_a, arrived[:, 0:IL]) + own_rows * gate_rows.astype(F32)
    new_conv = dot(take_b, arrived[:, 0:IL]) + own_rows * conv_rows.astype(F32)
    tail = dot(take_a, arrived[:, IL:])
    new_bc = tail[:, 0:GC] + own_rows * bc_rows.astype(F32)
    new_delta = tail[:, GC : GC + HL] + own_rows * delta_rows.astype(F32)

    gates[0:M] = gate_ref[0:PERIOD].reshape(M, IL).astype(F32)
    gates[M:] = new_gate

    seq = [conv_old[:, k, :] for k in range(3)]
    seq += [conv_ref[t].astype(F32) for t in range(PERIOD)]
    seq += [new_conv[k * S : (k + 1) * S] for k in range(moved)]
    for t in range(T):
        mixed = conv_b_ref[...]
        for k in range(4):
            mixed = mixed + conv_w_ref[k : k + 1, :] * seq[t + k]
        xs[t * S : (t + 1) * S] = silu(mixed)

    seq = [bc_old[:, k, :] for k in range(3)]
    seq += [bc_ref[t, :, group_cols].astype(F32) for t in range(PERIOD)]
    seq += [new_bc[k * S : (k + 1) * S] for k in range(moved)]
    for t in range(T):
        mixed = bc_b_ref[:, group_cols]
        for k in range(4):
            mixed = mixed + bc_w_ref[k : k + 1, group_cols] * seq[t + k]
        act = silu(mixed)
        for g in range(NG):
            low = g * 2 * STATE
            bs[t, :, g * STATE : (g + 1) * STATE] = act[:, low : low + STATE]
            cs[t, :, g * STATE : (g + 1) * STATE] = act[:, low + STATE : low + 2 * STATE]
    for t in range(T, 8):
        cs[t] = jnp.zeros((S, NG * STATE), F32)

    def one_slot(s, _):
        state_copy(s).wait()
        rows8 = cs[:, s, :]
        for g in range(NG):
            cg = rows8[:, g * STATE : (g + 1) * STATE]
            high = cg.astype(BF16).astype(F32)
            lhs = jnp.concatenate([high, cg - high], axis=0).astype(BF16)
            held = st[s, g * GH : (g + 1) * GH].reshape(GH * HEAD_DIM, STATE).astype(BF16)
            both = lax.dot_general(
                lhs, held, (((1,), (1,)), ((), ())), preferred_element_type=F32
            )
            y0[:, s, g * GH * HEAD_DIM : (g + 1) * GH * HEAD_DIM] = both[0:8] + both[8:16]
        return 0

    lax.fori_loop(0, S, one_slot, 0)

    finish = finish_ref[...]
    live = [jnp.where(finish > t, 1.0, 0.0) for t in range(T)]
    steps, keeps = [], []
    for t in range(T):
        if t < PERIOD:
            raw = delta_ref[t].astype(F32)
        else:
            raw = new_delta[(t - PERIOD) * S : (t - PERIOD + 1) * S]
        size = softplus(raw + delta_b_ref[...]) * live[t]
        steps.append(size)
        keeps.append(jnp.exp(-size * decay_ref[...]))

    head = lax.broadcasted_iota(jnp.int32, (S, HL), 1)
    spread_row = lax.broadcasted_iota(jnp.int32, (2 * HL, IL), 0)
    spread_col = lax.broadcasted_iota(jnp.int32, (2 * HL, IL), 1)
    spread_from = jnp.where(spread_row >= HL, spread_row - HL, spread_row) * HEAD_DIM
    offset = spread_col - spread_from
    spread = jnp.where((offset >= 0) & (offset < HEAD_DIM), 1.0, 0.0).astype(BF16)

    start = None
    weights = []
    lane = lax.broadcasted_iota(jnp.int32, (S, 128), 1)
    squares = jnp.zeros((S, 128), F32)
    for t in range(T):
        start = keeps[t] if t == 0 else start * keeps[t]
        weights = [w * keeps[t] for w in weights] + [steps[t]]
        blocks = [start]
        for u in range(t + 1):
            scores = jnp.zeros((S, HL), F32)
            for g in range(NG):
                span = slice(g * STATE, (g + 1) * STATE)
                score = jnp.sum(cs[t, :, span] * bs[u, :, span], axis=1, keepdims=True)
                inside = (head >= g * GH) & (head < (g + 1) * GH)
                scores = jnp.where(inside, score, scores)
            block = weights[u] * scores
            if u == t:
                block = block + skip_ref[...]
            blocks.append(block)
        table = jnp.concatenate(blocks, axis=0)
        high = table.astype(BF16).astype(F32)
        table = jnp.concatenate([high, table - high], axis=1).astype(BF16)
        width = min(IL, 512)
        square = jnp.zeros((S, 1), F32)
        for low in range(0, IL, width):
            cols = slice(low, low + width)
            wide = dot(table, spread[:, cols])
            total = wide[0:S] * y0[t, :, cols]
            for u in range(t + 1):
                total = total + wide[(u + 1) * S : (u + 2) * S] * xs[u * S : (u + 1) * S, cols]
            gated = total * silu(gates[t * S : (t + 1) * S, cols])
            square = square + jnp.sum(gated * gated, axis=1, keepdims=True)
            hidden[t * S : (t + 1) * S, cols] = (gated * gain_ref[:, cols]).astype(BF16)
        squares = jnp.where(lane == t, square, squares)

    sq_mine[...] = squares

    def sq_copy(o):
        return pltpu.make_async_remote_copy(
            src_ref=sq_mine,
            dst_ref=sq_got.at[o],
            send_sem=sq_send.at[o],
            recv_sem=sq_recv.at[o],
            device_id={"tp": lax.rem(tp + (o + 1), TP)},
            device_id_type=MESH,
        )

    for o in range(TP - 1):
        sq_copy(o).start()

    def part_copy(o):
        return pltpu.make_async_remote_copy(
            src_ref=part.at[o],
            dst_ref=part_got.at[o],
            send_sem=part_send.at[o],
            recv_sem=part_recv.at[o],
            device_id={"tp": lax.rem(tp + (o + 1), TP)},
            device_id_type=MESH,
        )

    for o in range(1, TP):
        w_copy(o).wait()
        part[o - 1] = dot(hidden[...], wv[o]).astype(BF16)
        part_copy(o - 1).start()
    w_copy(0).wait()
    total = dot(hidden[...], wv[0])

    for o in range(TP - 1):
        sq_copy(o).wait()
        squares = squares + sq_got[o]
    inv_rms = lax.rsqrt(squares / INNER + EPS)
    scale = jnp.concatenate([inv_rms[:, t : t + 1] * live[t] for t in range(T)], axis=0)

    for o in range(TP - 1):
        part_copy(o).wait()
        total = total + part_got[o].astype(F32)
    rows_out[...] = (total * scale).astype(BF16)

    half = DL // 2
    give_a, give_b = pack_matrix(S, moved, R - 1, give_send)
    later = rows_out[M:, :]
    packed = dot(give_a, later[:, 0:half]) + dot(give_b, later[:, half:])
    back[...] = packed.astype(BF16).reshape(R - 1, 16, half)

    def back_copy(o):
        return pltpu.make_async_remote_copy(
            src_ref=back.at[o],
            dst_ref=back_got.at[o],
            send_sem=back_send.at[o],
            recv_sem=back_recv.at[o],
            device_id={"rep": ahead(o)},
            device_id_type=MESH,
        )

    for o in range(R - 1):
        back_copy(o).start()
    out_ref[0:PERIOD] = rows_out[0:M, :].reshape(PERIOD, S, DL)
    put_a, put_b = unpack_matrix(S, moved, R - 1, give_take)
    keep = own * (1.0 - is_target)
    keep_rows = jnp.concatenate([keep] * moved, axis=0)
    stay = keep_rows * later.astype(F32)
    for o in range(R - 1):
        back_copy(o).wait()
    arrived = back_got[...].reshape((R - 1) * 16, half)
    left = (dot(put_a, arrived) + stay[:, 0:half]).astype(BF16)
    right = (dot(put_b, arrived) + stay[:, half:]).astype(BF16)
    out_ref[PERIOD:, :, 0:half] = left.reshape(moved, S, half)
    out_ref[PERIOD:, :, half:] = right.reshape(moved, S, half)


def body(R, TP, *arrays):
    (gate, conv, bc, delta, conv_w, conv_b, bc_w, bc_b, delta_b, decay, skip, gain, w, state,
     conv_state, bc_state, finish, plan) = arrays
    T, S, IL = gate.shape
    HL = delta.shape[2]
    NG = max(1, HL * GROUPS // HEADS)
    D = w.shape[1]
    DL = D // TP
    GC = NG * 2 * STATE
    wide = IL + GC + 128
    dims = (T, S, IL, HL, NG, R, TP, DL)
    vmem = pl.BlockSpec(memory_space=pltpu.VMEM)
    hbm = pl.BlockSpec(memory_space=pl.ANY)
    smem = pl.BlockSpec(memory_space=pltpu.SMEM)
    dma = pltpu.SemaphoreType.DMA
    half = DL // 2
    return pl.pallas_call(
        functools.partial(kernel, dims),
        out_shape=jax.ShapeDtypeStruct((T, S, DL), BF16),
        in_specs=[vmem] * 12 + [hbm, hbm] + [vmem] * 3 + [smem],
        out_specs=vmem,
        scratch_shapes=[
            pltpu.VMEM((S, HL, HEAD_DIM, STATE), F32),
            pltpu.VMEM((TP, IL, DL), BF16),
            pltpu.VMEM((R - 1, 16, wide), BF16),
            pltpu.VMEM((R - 1, 16, wide), BF16),
            pltpu.VMEM((T * S, IL), F32),
            pltpu.VMEM((8, S, NG * STATE), F32),
            pltpu.VMEM((8, S, NG * STATE), F32),
            pltpu.VMEM((8, S, IL), F32),
            pltpu.VMEM((T * S, IL), F32),
            pltpu.VMEM((T * S, IL), BF16),
            pltpu.VMEM((S, 128), F32),
            pltpu.VMEM((TP - 1, S, 128), F32),
            pltpu.VMEM((TP - 1, T * S, DL), BF16),
            pltpu.VMEM((TP - 1, T * S, DL), BF16),
            pltpu.VMEM((T * S, DL), BF16),
            pltpu.VMEM((R - 1, 16, half), BF16),
            pltpu.VMEM((R - 1, 16, half), BF16),
            dma((S,)),
            dma((TP,)),
            dma((R - 1,)),
            dma((R - 1,)),
            dma((TP - 1,)),
            dma((TP - 1,)),
            dma((TP - 1,)),
            dma((TP - 1,)),
            dma((R - 1,)),
            dma((R - 1,)),
        ],
        compiler_params=pltpu.CompilerParams(
            collective_id=0, has_side_effects=True, vmem_limit_bytes=58 * 1024 * 1024
        ),
    )(
        gate,
        conv,
        bc,
        delta,
        conv_w,
        conv_b.reshape(1, -1),
        bc_w,
        bc_b.reshape(1, -1),
        delta_b.reshape(1, -1),
        decay.reshape(1, -1),
        skip.reshape(1, -1),
        gain.reshape(1, -1),
        w,
        state,
        conv_state,
        bc_state,
        finish.reshape(-1, 1),
        plan.reshape(-1),
    )


def solution(mesh):
    rows = ("parts", "rep")
    in_specs = (
        P(None, rows, "tp"),
        P(None, rows, "tp"),
        P(None, rows, None),
        P(None, rows, "tp"),
        P(None, "tp"),
        P("tp"),
        P(),
        P(),
        P("tp"),
        P("tp"),
        P("tp"),
        P("tp"),
        P("tp", None),
        P(rows, "tp", None, None),
        P(rows, None, "tp"),
        P(rows, None, None),
        P(rows),
        P("parts", None, None, None, None),
    )
    return jax.shard_map(
        functools.partial(body, mesh.shape["rep"], mesh.shape["tp"]),
        mesh=mesh,
        in_specs=in_specs,
        out_specs=P(None, rows, "tp"),
        check_vma=False,
    )
```

```python
import functools

import jax
import jax.numpy as jnp
from jax import lax
from jax.experimental import pallas as pl
from jax.experimental.pallas import tpu as pltpu
from jax.sharding import PartitionSpec as P

HEADS = 128
HEAD_DIM = 64
STATE = 128
GROUPS = 8
PERIOD = 3
CAP = 2
INNER = 8192
EPS = 1e-05
BF16 = jnp.bfloat16
F32 = jnp.float32
MESH = pl.DeviceIdType.MESH


def silu(v):
    return v / (1.0 + jnp.exp(-v))


def softplus(v):
    return jnp.maximum(v, 0.0) + jnp.log1p(jnp.exp(-jnp.abs(v)))


def dot(a, b):
    return lax.dot_general(a, b, (((1,), (0,)), ((), ())), preferred_element_type=F32)


def pack_matrix(slots, moved, peers, pick):
    rows, cols = 16 * peers, moved * slots
    row = lax.broadcasted_iota(jnp.int32, (rows, cols), 0)
    col = lax.broadcasted_iota(jnp.int32, (rows, cols), 1)
    halves = []
    for half in range(2):
        hit = jnp.zeros((rows, cols), F32)
        for o in range(peers):
            for c in range(CAP):
                slot = pick(o, c)
                first = o * 16 + half * CAP * moved + c * moved
                for k in range(moved):
                    match = jnp.where(row == first + k, col, -1) == k * slots + slot
                    valid = jnp.where(slot >= 0, 1.0, 0.0)
                    hit = hit + jnp.where(match, valid, 0.0)
        halves.append(hit.astype(BF16))
    return halves


def unpack_matrix(slots, moved, peers, pick):
    rows, cols = moved * slots, 16 * peers
    row = lax.broadcasted_iota(jnp.int32, (rows, cols), 0)
    col = lax.broadcasted_iota(jnp.int32, (rows, cols), 1)
    halves = []
    for half in range(2):
        hit = jnp.zeros((rows, cols), F32)
        for o in range(peers):
            for c in range(CAP):
                slot = pick(o, c)
                first = o * 16 + half * CAP * moved + c * moved
                for k in range(moved):
                    match = jnp.where(col == first + k, row, -1) == k * slots + slot
                    valid = jnp.where(slot >= 0, 1.0, 0.0)
                    hit = hit + jnp.where(match, valid, 0.0)
        halves.append(hit.astype(BF16))
    return halves


def named(slots, peers, pick):
    row = lax.broadcasted_iota(jnp.int32, (slots, 1), 0)
    hit = jnp.zeros((slots, 1), F32)
    for o in range(peers):
        for c in range(CAP):
            hit = jnp.maximum(hit, jnp.where(row == pick(o, c), 1.0, 0.0))
    return hit


def kernel(
    dims,
    gate_ref,
    conv_ref,
    bc_ref,
    delta_ref,
    conv_w_ref,
    conv_b_ref,
    bc_w_ref,
    bc_b_ref,
    delta_b_ref,
    decay_ref,
    skip_ref,
    gain_ref,
    w_hbm,
    state_hbm,
    conv_state_ref,
    bc_state_ref,
    finish_ref,
    plan_ref,
    out_ref,
    st,
    wv,
    msg,
    got,
    xs,
    bs,
    cs,
    y0,
    new_gates,
    hidden,
    sq_mine,
    sq_got,
    own_part,
    part,
    part_got,
    back,
    back_got,
    st_sem,
    w_sem,
    msg_send,
    msg_recv,
    sq_send,
    sq_recv,
    part_send,
    part_recv,
    back_send,
    back_recv,
):
    T, S, IL, HL, NG, R, TP, DL = dims
    GH = HL // NG
    GC = NG * 2 * STATE
    moved = T - PERIOD
    M = moved * S
    me = lax.axis_index("rep")
    tp = lax.axis_index("tp")

    def state_copy(s):
        return pltpu.make_async_copy(state_hbm.at[s], st.at[s], st_sem.at[s])

    def w_copy(o):
        column = pl.multiple_of(lax.rem(tp + o, TP) * DL, DL)
        return pltpu.make_async_copy(w_hbm.at[:, pl.ds(column, DL)], wv.at[o], w_sem.at[o])

    barrier = pltpu.get_barrier_semaphore()
    for o in range(1, R):
        pl.semaphore_signal(
            barrier, inc=1, device_id={"rep": lax.rem(me + o, R)}, device_id_type=MESH
        )
    for o in range(1, TP):
        pl.semaphore_signal(
            barrier, inc=1, device_id={"tp": lax.rem(tp + o, TP)}, device_id_type=MESH
        )

    for s in range(S):
        state_copy(s).start()
    for o in list(range(1, TP)) + [0]:
        w_copy(o).start()

    def entry(source, target, c, which):
        return plan_ref[source * CAP + c, which, target]

    def ahead(o):
        return lax.rem(me + (o + 1), R)

    def behind(o):
        return lax.rem(me + (R - 1 - o), R)

    serve_send = lambda o, c: entry(ahead(o), me, c, 1)
    serve_take = lambda o, c: entry(me, behind(o), c, 0)
    give_send = lambda o, c: entry(me, ahead(o), c, 0)
    give_take = lambda o, c: entry(behind(o), me, c, 1)

    group_column = pl.multiple_of((tp * HL * GROUPS // HEADS) * 2 * STATE, 2 * STATE)
    group_cols = pl.ds(group_column, GC)

    pack_a, pack_b = pack_matrix(S, moved, R - 1, serve_send)
    gate_rows = gate_ref[PERIOD:].reshape(M, IL)
    conv_rows = conv_ref[PERIOD:].reshape(M, IL)
    bc_rows = bc_ref[PERIOD:, :, group_cols].reshape(M, GC)
    delta_rows = delta_ref[PERIOD:].reshape(M, HL)
    packed = dot(pack_a, gate_rows) + dot(pack_b, conv_rows)
    msg[:, :, 0:IL] = packed.astype(BF16).reshape(R - 1, 16, IL)
    msg[:, :, IL : IL + GC] = dot(pack_a, bc_rows).astype(BF16).reshape(R - 1, 16, GC)
    pad_rows = jnp.concatenate([delta_rows.astype(F32), jnp.zeros((M, 128 - HL), F32)], axis=1)
    msg[:, :, IL + GC :] = dot(pack_a, pad_rows.astype(BF16)).astype(BF16).reshape(R - 1, 16, 128)

    pl.semaphore_wait(barrier, R - 1 + TP - 1)

    def msg_copy(o):
        return pltpu.make_async_remote_copy(
            src_ref=msg.at[o],
            dst_ref=got.at[o],
            send_sem=msg_send.at[o],
            recv_sem=msg_recv.at[o],
            device_id={"rep": ahead(o)},
            device_id_type=MESH,
        )

    for o in range(R - 1):
        msg_copy(o).start()

    def sq_copy(h, o):
        return pltpu.make_async_remote_copy(
            src_ref=sq_mine.at[h],
            dst_ref=sq_got.at[h, o],
            send_sem=sq_send.at[h, o],
            recv_sem=sq_recv.at[h, o],
            device_id={"tp": lax.rem(tp + (o + 1), TP)},
            device_id_type=MESH,
        )

    def part_copy(h, o):
        return pltpu.make_async_remote_copy(
            src_ref=part.at[h, o],
            dst_ref=part_got.at[h, o],
            send_sem=part_send.at[h, o],
            recv_sem=part_recv.at[h, o],
            device_id={"tp": lax.rem(tp + (o + 1), TP)},
            device_id_type=MESH,
        )

    slot_row = lax.broadcasted_iota(jnp.int32, (S, 1), 0)
    finish = jnp.zeros((S, 1), jnp.int32)
    for s in range(S):
        finish = jnp.where(slot_row == s, finish_ref[s], finish)
    live = [jnp.where(finish > t, 1.0, 0.0) for t in range(T)]

    head = lax.broadcasted_iota(jnp.int32, (S, HL), 1)
    lane = lax.broadcasted_iota(jnp.int32, (S, 128), 1)
    spread_row = lax.broadcasted_iota(jnp.int32, (2 * HL, IL), 0)
    spread_col = lax.broadcasted_iota(jnp.int32, (2 * HL, IL), 1)
    spread_from = jnp.where(spread_row >= HL, spread_row - HL, spread_row) * HEAD_DIM
    offset = spread_col - spread_from
    spread = jnp.where((offset >= 0) & (offset < HEAD_DIM), 1.0, 0.0).astype(BF16)

    def convolve(h, ts, seq, bc_seq):
        for t in ts:
            mixed = conv_b_ref[...]
            for k in range(4):
                mixed = mixed + conv_w_ref[k : k + 1, :] * seq[t + k]
            xs[t * S : (t + 1) * S] = silu(mixed)
            mixed = bc_b_ref[:, group_cols]
            for k in range(4):
                mixed = mixed + bc_w_ref[k : k + 1, group_cols] * bc_seq[t + k]
            act = silu(mixed)
            for g in range(NG):
                low = g * 2 * STATE
                row = t - ts[0]
                bs[t, :, g * STATE : (g + 1) * STATE] = act[:, low : low + STATE]
                cs[h, row, :, g * STATE : (g + 1) * STATE] = act[:, low + STATE : low + 2 * STATE]
        for row in range(len(ts), 8):
            cs[h, row] = jnp.zeros((S, NG * STATE), F32)

    def contract(h, count):
        batch = 4 if S % 4 == 0 else 1

        def some_slots(i, _):
            if h == 0:
                for b in range(batch):
                    state_copy(i * batch + b).wait()
            for b in range(batch):
                s = i * batch + b
                rows8 = cs[h, :, s, :]
                for g in range(NG):
                    cg = rows8[:, g * STATE : (g + 1) * STATE]
                    high = cg.astype(BF16).astype(F32)
                    lhs = jnp.concatenate([high, cg - high], axis=0).astype(BF16)
                    held = st[s, g * GH : (g + 1) * GH].reshape(GH * HEAD_DIM, STATE).astype(BF16)
                    both = lax.dot_general(
                        lhs, held, (((1,), (1,)), ((), ())), preferred_element_type=F32
                    )
                    value = both[0:count] + both[8 : 8 + count]
                    y0[0:count, s, g * GH * HEAD_DIM : (g + 1) * GH * HEAD_DIM] = value
            return 0

        lax.fori_loop(0, S // batch, some_slots, 0)

    carry = {"start": None, "weights": []}

    def combine(h, ts, raw_of, gate_of):
        squares = jnp.zeros((S, 128), F32)
        for t in ts:
            row = t - ts[0]
            size = softplus(raw_of(t) + delta_b_ref[...]) * live[t]
            keep = jnp.exp(-size * decay_ref[...])
            carry["start"] = keep if t == 0 else carry["start"] * keep
            carry["weights"] = [w * keep for w in carry["weights"]] + [size]
            blocks = [carry["start"]]
            for u in range(t + 1):
                scores = jnp.zeros((S, HL), F32)
                for g in range(NG):
                    span = slice(g * STATE, (g + 1) * STATE)
                    score = jnp.sum(cs[h, row, :, span] * bs[u, :, span], axis=1, keepdims=True)
                    inside = (head >= g * GH) & (head < (g + 1) * GH)
                    scores = jnp.where(inside, score, scores)
                block = carry["weights"][u] * scores
                if u == t:
                    block = block + skip_ref[...]
                blocks.append(block)
            table = jnp.concatenate(blocks, axis=0)
            high = table.astype(BF16).astype(F32)
            table = jnp.concatenate([high, table - high], axis=1).astype(BF16)
            width = min(IL, 512)
            square = jnp.zeros((S, 1), F32)
            for low in range(0, IL, width):
                cols = slice(low, low + width)
                wide = dot(table, spread[:, cols])
                total = wide[0:S] * y0[row, :, cols]
                for u in range(t + 1):
                    total = total + wide[(u + 1) * S : (u + 2) * S] * xs[u * S : (u + 1) * S, cols]
                gated = total * silu(gate_of(t, cols))
                square = square + jnp.sum(gated * gated, axis=1, keepdims=True)
                hidden[h, row * S : (row + 1) * S, cols] = (gated * gain_ref[:, cols]).astype(BF16)
            squares = jnp.where(lane == t, square, squares)
        sq_mine[h] = squares
        for o in range(TP - 1):
            sq_copy(h, o).start()

    def project(h):
        for o in range(1, TP):
            if h == 0:
                w_copy(o).wait()
            part[h, o - 1] = dot(hidden[h], wv[o]).astype(BF16)
            part_copy(h, o - 1).start()
        if h == 0:
            w_copy(0).wait()
        own_part[h] = dot(hidden[h], wv[0])

    def finish_half(h, ts):
        squares = sq_mine[h]
        for o in range(TP - 1):
            sq_copy(h, o).wait()
            squares = squares + sq_got[h, o]
        inv_rms = lax.rsqrt(squares / INNER + EPS)
        scale = jnp.concatenate([inv_rms[:, t : t + 1] * live[t] for t in ts], axis=0)
        total = own_part[h]
        for o in range(TP - 1):
            part_copy(h, o).wait()
            total = total + part_got[h, o].astype(F32)
        return (total * scale).astype(BF16)

    early, late = list(range(PERIOD)), list(range(PERIOD, T))
    seq = [conv_state_ref[k].astype(F32) for k in range(3)]
    seq += [conv_ref[t].astype(F32) for t in early]
    bc_seq = [bc_state_ref[k, :, group_cols].astype(F32) for k in range(3)]
    bc_seq += [bc_ref[t, :, group_cols].astype(F32) for t in early]
    convolve(0, early, seq, bc_seq)
    contract(0, PERIOD)
    combine(
        0,
        early,
        lambda t: delta_ref[t].astype(F32),
        lambda t, cols: gate_ref[t, :, cols].astype(F32),
    )
    project(0)

    take_a, take_b = unpack_matrix(S, moved, R - 1, serve_take)
    own = 1.0 - named(S, R - 1, serve_take)
    own_rows = jnp.concatenate([own] * moved, axis=0)
    for o in range(R - 1):
        msg_copy(o).wait()
    arrived = got[...].reshape((R - 1) * 16, IL + GC + 128)
    new_gates[...] = dot(take_a, arrived[:, 0:IL]) + own_rows * gate_rows.astype(F32)
    new_conv = dot(take_b, arrived[:, 0:IL]) + own_rows * conv_rows.astype(F32)
    tail = dot(take_a, arrived[:, IL:])
    new_bc = tail[:, 0:GC] + own_rows * bc_rows.astype(F32)
    new_delta = tail[:, GC : GC + HL] + own_rows * delta_rows.astype(F32)
    seq = [conv_ref[t].astype(F32) if t < PERIOD else None for t in range(PERIOD)]
    seq = [None] * 3 + seq + [new_conv[k * S : (k + 1) * S] for k in range(moved)]
    bc_seq = [None] * 3 + [bc_ref[t, :, group_cols].astype(F32) for t in range(PERIOD)]
    bc_seq += [new_bc[k * S : (k + 1) * S] for k in range(moved)]
    convolve(1, late, seq, bc_seq)
    contract(1, moved)
    combine(
        1,
        late,
        lambda t: new_delta[(t - PERIOD) * S : (t - PERIOD + 1) * S],
        lambda t, cols: new_gates[(t - PERIOD) * S : (t - PERIOD + 1) * S, cols],
    )
    project(1)

    out_ref[0:PERIOD] = finish_half(0, early).reshape(PERIOD, S, DL)
    half = DL // 2
    give_a, give_b = pack_matrix(S, moved, R - 1, give_send)
    put_a, put_b = unpack_matrix(S, moved, R - 1, give_take)
    is_target = named(S, R - 1, give_take)
    keep_rows = jnp.concatenate([own * (1.0 - is_target)] * moved, axis=0)

    later = finish_half(1, late)
    packed = dot(give_a, later[:, 0:half]) + dot(give_b, later[:, half:])
    back[...] = packed.astype(BF16).reshape(R - 1, 16, half)

    def back_copy(o):
        return pltpu.make_async_remote_copy(
            src_ref=back.at[o],
            dst_ref=back_got.at[o],
            send_sem=back_send.at[o],
            recv_sem=back_recv.at[o],
            device_id={"rep": ahead(o)},
            device_id_type=MESH,
        )

    for o in range(R - 1):
        back_copy(o).start()
    stay = keep_rows * later.astype(F32)
    for o in range(R - 1):
        back_copy(o).wait()
    arrived = back_got[...].reshape((R - 1) * 16, half)
    left = (dot(put_a, arrived) + stay[:, 0:half]).astype(BF16)
    right = (dot(put_b, arrived) + stay[:, half:]).astype(BF16)
    out_ref[PERIOD:, :, 0:half] = left.reshape(moved, S, half)
    out_ref[PERIOD:, :, half:] = right.reshape(moved, S, half)


def body(R, TP, *arrays):
    (gate, conv, bc, delta, conv_w, conv_b, bc_w, bc_b, delta_b, decay, skip, gain, w, state,
     conv_state, bc_state, finish, plan) = arrays
    T, S, IL = gate.shape
    HL = delta.shape[2]
    NG = max(1, HL * GROUPS // HEADS)
    D = w.shape[1]
    DL = D // TP
    GC = NG * 2 * STATE
    wide = IL + GC + 128
    dims = (T, S, IL, HL, NG, R, TP, DL)
    vmem = pl.BlockSpec(memory_space=pltpu.VMEM)
    hbm = pl.BlockSpec(memory_space=pl.ANY)
    smem = pl.BlockSpec(memory_space=pltpu.SMEM)
    dma = pltpu.SemaphoreType.DMA
    half = DL // 2
    rows = PERIOD * S
    return pl.pallas_call(
        functools.partial(kernel, dims),
        out_shape=jax.ShapeDtypeStruct((T, S, DL), BF16),
        in_specs=[vmem] * 12 + [hbm, hbm] + [vmem] * 2 + [smem] * 2,
        out_specs=vmem,
        scratch_shapes=[
            pltpu.VMEM((S, HL, HEAD_DIM, STATE), F32),
            pltpu.VMEM((TP, IL, DL), BF16),
            pltpu.VMEM((R - 1, 16, wide), BF16),
            pltpu.VMEM((R - 1, 16, wide), BF16),
            pltpu.VMEM((T * S, IL), F32),
            pltpu.VMEM((T, S, NG * STATE), F32),
            pltpu.VMEM((2, 8, S, NG * STATE), F32),
            pltpu.VMEM((rows // S, S, IL), F32),
            pltpu.VMEM((rows, IL), F32),
            pltpu.VMEM((2, rows, IL), BF16),
            pltpu.VMEM((2, S, 128), F32),
            pltpu.VMEM((2, TP - 1, S, 128), F32),
            pltpu.VMEM((2, rows, DL), F32),
            pltpu.VMEM((2, TP - 1, rows, DL), BF16),
            pltpu.VMEM((2, TP - 1, rows, DL), BF16),
            pltpu.VMEM((R - 1, 16, half), BF16),
            pltpu.VMEM((R - 1, 16, half), BF16),
            dma((S,)),
            dma((TP,)),
            dma((R - 1,)),
            dma((R - 1,)),
            dma((2, TP - 1)),
            dma((2, TP - 1)),
            dma((2, TP - 1)),
            dma((2, TP - 1)),
            dma((R - 1,)),
            dma((R - 1,)),
        ],
        compiler_params=pltpu.CompilerParams(
            collective_id=0, has_side_effects=True, vmem_limit_bytes=58 * 1024 * 1024
        ),
    )(
        gate,
        conv,
        bc,
        delta,
        conv_w,
        conv_b.reshape(1, -1),
        bc_w,
        bc_b.reshape(1, -1),
        delta_b.reshape(1, -1),
        decay.reshape(1, -1),
        skip.reshape(1, -1),
        gain.reshape(1, -1),
        w,
        state,
        conv_state.transpose(1, 0, 2),
        bc_state.transpose(1, 0, 2),
        finish,
        plan.transpose(0, 1, 3, 4, 2).reshape(R * CAP, 2, R),
    )


def solution(mesh):
    rows = ("parts", "rep")
    in_specs = (
        P(None, rows, "tp"),
        P(None, rows, "tp"),
        P(None, rows, None),
        P(None, rows, "tp"),
        P(None, "tp"),
        P("tp"),
        P(),
        P(),
        P("tp"),
        P("tp"),
        P("tp"),
        P("tp"),
        P("tp", None),
        P(rows, "tp", None, None),
        P(rows, None, "tp"),
        P(rows, None, None),
        P(rows),
        P("parts", None, None, None, None),
    )
    return jax.shard_map(
        functools.partial(body, mesh.shape["rep"], mesh.shape["tp"]),
        mesh=mesh,
        in_specs=in_specs,
        out_specs=P(None, rows, "tp"),
        check_vma=False,
    )
```

```python
import functools

import jax
import jax.numpy as jnp
from jax import lax
from jax.experimental import pallas as pl
from jax.experimental.pallas import tpu as pltpu
from jax.sharding import PartitionSpec as P

HEADS = 128
HEAD_DIM = 64
STATE = 128
GROUPS = 8
PERIOD = 3
CAP = 2
INNER = 8192
EPS = 1e-05
BF16 = jnp.bfloat16
F32 = jnp.float32
MESH = pl.DeviceIdType.MESH


def silu(v):
    return v / (1.0 + jnp.exp(-v))


def softplus(v):
    return jnp.maximum(v, 0.0) + jnp.log1p(jnp.exp(-jnp.abs(v)))


def dot(a, b):
    return lax.dot_general(a, b, (((1,), (0,)), ((), ())), preferred_element_type=F32)


def pack_matrix(slots, moved, peers, pick):
    rows, cols = 16 * peers, moved * slots
    row = lax.broadcasted_iota(jnp.int32, (rows, cols), 0)
    col = lax.broadcasted_iota(jnp.int32, (rows, cols), 1)
    halves = []
    for half in range(2):
        hit = jnp.zeros((rows, cols), F32)
        for o in range(peers):
            for c in range(CAP):
                slot = pick(o, c)
                first = o * 16 + half * CAP * moved + c * moved
                for k in range(moved):
                    match = jnp.where(row == first + k, col, -1) == k * slots + slot
                    valid = jnp.where(slot >= 0, 1.0, 0.0)
                    hit = hit + jnp.where(match, valid, 0.0)
        halves.append(hit.astype(BF16))
    return halves


def unpack_matrix(slots, moved, peers, pick):
    rows, cols = moved * slots, 16 * peers
    row = lax.broadcasted_iota(jnp.int32, (rows, cols), 0)
    col = lax.broadcasted_iota(jnp.int32, (rows, cols), 1)
    halves = []
    for half in range(2):
        hit = jnp.zeros((rows, cols), F32)
        for o in range(peers):
            for c in range(CAP):
                slot = pick(o, c)
                first = o * 16 + half * CAP * moved + c * moved
                for k in range(moved):
                    match = jnp.where(col == first + k, row, -1) == k * slots + slot
                    valid = jnp.where(slot >= 0, 1.0, 0.0)
                    hit = hit + jnp.where(match, valid, 0.0)
        halves.append(hit.astype(BF16))
    return halves


def named(slots, peers, pick):
    row = lax.broadcasted_iota(jnp.int32, (slots, 1), 0)
    hit = jnp.zeros((slots, 1), F32)
    for o in range(peers):
        for c in range(CAP):
            hit = jnp.maximum(hit, jnp.where(row == pick(o, c), 1.0, 0.0))
    return hit


def kernel(
    dims,
    gate_ref,
    conv_ref,
    bc_ref,
    delta_ref,
    conv_w_ref,
    conv_b_ref,
    bc_w_ref,
    bc_b_ref,
    delta_b_ref,
    decay_ref,
    skip_ref,
    gain_ref,
    w_hbm,
    state_hbm,
    conv_state_ref,
    bc_state_ref,
    finish_ref,
    plan_ref,
    out_ref,
    st,
    wv,
    msg,
    got,
    xs,
    bs,
    cs,
    y0,
    new_gates,
    hidden,
    sq_mine,
    sq_got,
    own_part,
    part,
    part_got,
    back,
    back_got,
    st_sem,
    w_sem,
    msg_send,
    msg_recv,
    sq_send,
    sq_recv,
    part_send,
    part_recv,
    back_send,
    back_recv,
):
    T, S, IL, HL, NG, R, TP, DL = dims
    GH = HL // NG
    GC = NG * 2 * STATE
    moved = T - PERIOD
    M = moved * S
    me = lax.axis_index("rep")
    tp = lax.axis_index("tp")

    stages = TP.bit_length() - 1
    by_stage = [[m for m in reversed(range(1, TP)) if m & -m == 1 << k] for k in range(stages)]

    def flipped(mask):
        index = tp
        for k in range(stages):
            if mask >> k & 1:
                bit = lax.rem(tp // (1 << k), 2)
                index = index + (1 << k) * (1 - 2 * bit)
        return index

    def state_copy(s):
        return pltpu.make_async_copy(state_hbm.at[s], st.at[s], st_sem.at[s])

    def w_copy(o):
        column = pl.multiple_of(flipped(o) * DL, DL)
        return pltpu.make_async_copy(w_hbm.at[:, pl.ds(column, DL)], wv.at[o], w_sem.at[o])

    barrier = pltpu.get_barrier_semaphore()
    for o in range(1, R):
        pl.semaphore_signal(
            barrier, inc=1, device_id={"rep": lax.rem(me + o, R)}, device_id_type=MESH
        )
    for o in range(1, TP):
        pl.semaphore_signal(
            barrier, inc=1, device_id={"tp": lax.rem(tp + o, TP)}, device_id_type=MESH
        )

    for s in range(S):
        state_copy(s).start()
    for m in sum(by_stage, []) + [0]:
        w_copy(m).start()

    def entry(source, target, c, which):
        return plan_ref[source * CAP + c, which, target]

    def ahead(o):
        return lax.rem(me + (o + 1), R)

    def behind(o):
        return lax.rem(me + (R - 1 - o), R)

    serve_send = lambda o, c: entry(ahead(o), me, c, 1)
    serve_take = lambda o, c: entry(me, behind(o), c, 0)
    give_send = lambda o, c: entry(me, ahead(o), c, 0)
    give_take = lambda o, c: entry(behind(o), me, c, 1)

    group_column = pl.multiple_of((tp * HL * GROUPS // HEADS) * 2 * STATE, 2 * STATE)
    group_cols = pl.ds(group_column, GC)

    pack_a, pack_b = pack_matrix(S, moved, R - 1, serve_send)
    gate_rows = gate_ref[PERIOD:].reshape(M, IL)
    conv_rows = conv_ref[PERIOD:].reshape(M, IL)
    bc_rows = bc_ref[PERIOD:, :, group_cols].reshape(M, GC)
    delta_rows = delta_ref[PERIOD:].reshape(M, HL)
    packed = dot(pack_a, gate_rows) + dot(pack_b, conv_rows)
    msg[:, :, 0:IL] = packed.astype(BF16).reshape(R - 1, 16, IL)
    msg[:, :, IL : IL + GC] = dot(pack_a, bc_rows).astype(BF16).reshape(R - 1, 16, GC)
    pad_rows = jnp.concatenate([delta_rows.astype(F32), jnp.zeros((M, 128 - HL), F32)], axis=1)
    msg[:, :, IL + GC :] = dot(pack_a, pad_rows.astype(BF16)).astype(BF16).reshape(R - 1, 16, 128)

    pl.semaphore_wait(barrier, R - 1 + TP - 1)

    def msg_copy(o):
        return pltpu.make_async_remote_copy(
            src_ref=msg.at[o],
            dst_ref=got.at[o],
            send_sem=msg_send.at[o],
            recv_sem=msg_recv.at[o],
            device_id={"rep": ahead(o)},
            device_id_type=MESH,
        )

    for o in range(R - 1):
        msg_copy(o).start()

    def sq_copy(h, o):
        return pltpu.make_async_remote_copy(
            src_ref=sq_mine.at[h],
            dst_ref=sq_got.at[h, o],
            send_sem=sq_send.at[h, o],
            recv_sem=sq_recv.at[h, o],
            device_id={"tp": lax.rem(tp + (o + 1), TP)},
            device_id_type=MESH,
        )

    def part_copy(h, m):
        return pltpu.make_async_remote_copy(
            src_ref=part.at[h, m],
            dst_ref=part_got.at[h, m],
            send_sem=part_send.at[h, m],
            recv_sem=part_recv.at[h, m],
            device_id={"tp": flipped(m & -m)},
            device_id_type=MESH,
        )

    slot_row = lax.broadcasted_iota(jnp.int32, (S, 1), 0)
    finish = jnp.zeros((S, 1), jnp.int32)
    for s in range(S):
        finish = jnp.where(slot_row == s, finish_ref[s], finish)
    live = [jnp.where(finish > t, 1.0, 0.0) for t in range(T)]

    head = lax.broadcasted_iota(jnp.int32, (S, HL), 1)
    lane = lax.broadcasted_iota(jnp.int32, (S, 128), 1)
    spread_row = lax.broadcasted_iota(jnp.int32, (2 * HL, IL), 0)
    spread_col = lax.broadcasted_iota(jnp.int32, (2 * HL, IL), 1)
    spread_from = jnp.where(spread_row >= HL, spread_row - HL, spread_row) * HEAD_DIM
    offset = spread_col - spread_from
    spread = jnp.where((offset >= 0) & (offset < HEAD_DIM), 1.0, 0.0).astype(BF16)

    def convolve(h, ts, seq, bc_seq):
        for t in ts:
            mixed = conv_b_ref[...]
            for k in range(4):
                mixed = mixed + conv_w_ref[k : k + 1, :] * seq[t + k]
            xs[t * S : (t + 1) * S] = silu(mixed)
            mixed = bc_b_ref[:, group_cols]
            for k in range(4):
                mixed = mixed + bc_w_ref[k : k + 1, group_cols] * bc_seq[t + k]
            act = silu(mixed)
            for g in range(NG):
                low = g * 2 * STATE
                row = t - ts[0]
                bs[t, :, g * STATE : (g + 1) * STATE] = act[:, low : low + STATE]
                cs[h, row, :, g * STATE : (g + 1) * STATE] = act[:, low + STATE : low + 2 * STATE]
        for row in range(len(ts), 8):
            cs[h, row] = jnp.zeros((S, NG * STATE), F32)

    def contract(h, count):
        batch = 4 if S % 4 == 0 else 1

        def some_slots(i, _):
            if h == 0:
                for b in range(batch):
                    state_copy(i * batch + b).wait()
            for b in range(batch):
                s = i * batch + b
                rows8 = cs[h, :, s, :]
                for g in range(NG):
                    cg = rows8[:, g * STATE : (g + 1) * STATE]
                    high = cg.astype(BF16).astype(F32)
                    lhs = jnp.concatenate([high, cg - high], axis=0).astype(BF16)
                    held = st[s, g * GH : (g + 1) * GH].reshape(GH * HEAD_DIM, STATE).astype(BF16)
                    both = lax.dot_general(
                        lhs, held, (((1,), (1,)), ((), ())), preferred_element_type=F32
                    )
                    value = both[0:count] + both[8 : 8 + count]
                    y0[0:count, s, g * GH * HEAD_DIM : (g + 1) * GH * HEAD_DIM] = value
            return 0

        lax.fori_loop(0, S // batch, some_slots, 0)

    carry = {"start": None, "weights": []}

    def combine(h, ts, raw_of, gate_of):
        squares = jnp.zeros((S, 128), F32)
        for t in ts:
            row = t - ts[0]
            size = softplus(raw_of(t) + delta_b_ref[...]) * live[t]
            keep = jnp.exp(-size * decay_ref[...])
            carry["start"] = keep if t == 0 else carry["start"] * keep
            carry["weights"] = [w * keep for w in carry["weights"]] + [size]
            blocks = [carry["start"]]
            for u in range(t + 1):
                scores = jnp.zeros((S, HL), F32)
                for g in range(NG):
                    span = slice(g * STATE, (g + 1) * STATE)
                    score = jnp.sum(cs[h, row, :, span] * bs[u, :, span], axis=1, keepdims=True)
                    inside = (head >= g * GH) & (head < (g + 1) * GH)
                    scores = jnp.where(inside, score, scores)
                block = carry["weights"][u] * scores
                if u == t:
                    block = block + skip_ref[...]
                blocks.append(block)
            table = jnp.concatenate(blocks, axis=0)
            high = table.astype(BF16).astype(F32)
            table = jnp.concatenate([high, table - high], axis=1).astype(BF16)
            width = min(IL, 512)
            square = jnp.zeros((S, 1), F32)
            for low in range(0, IL, width):
                cols = slice(low, low + width)
                wide = dot(table, spread[:, cols])
                total = wide[0:S] * y0[row, :, cols]
                for u in range(t + 1):
                    total = total + wide[(u + 1) * S : (u + 2) * S] * xs[u * S : (u + 1) * S, cols]
                gated = total * silu(gate_of(t, cols))
                square = square + jnp.sum(gated * gated, axis=1, keepdims=True)
                hidden[h, row * S : (row + 1) * S, cols] = (gated * gain_ref[:, cols]).astype(BF16)
            squares = jnp.where(lane == t, square, squares)
        sq_mine[h] = squares
        for o in range(TP - 1):
            sq_copy(h, o).start()

    def project(h):
        for k in range(stages):
            for m in by_stage[k]:
                if h == 0:
                    w_copy(m).wait()
                block = dot(hidden[h], wv[m])
                if k == 0:
                    part[h, m] = block.astype(BF16)
                    part_copy(h, m).start()
                else:
                    own_part[h, m] = block
        if h == 0:
            w_copy(0).wait()
        own_part[h, 0] = dot(hidden[h], wv[0])

    def relay(h):
        for k in range(1, stages):
            for m in by_stage[k - 1]:
                part_copy(h, m).wait()
                kept = m - (1 << (k - 1))
                block = own_part[h, kept] + part_got[h, m].astype(F32)
                if kept in by_stage[k]:
                    part[h, kept] = block.astype(BF16)
                    part_copy(h, kept).start()
                else:
                    own_part[h, kept] = block

    def finish_half(h, ts):
        squares = sq_mine[h]
        for o in range(TP - 1):
            sq_copy(h, o).wait()
            squares = squares + sq_got[h, o]
        inv_rms = lax.rsqrt(squares / INNER + EPS)
        scale = jnp.concatenate([inv_rms[:, t : t + 1] * live[t] for t in ts], axis=0)
        total = own_part[h, 0]
        if stages:
            last = 1 << (stages - 1)
            part_copy(h, last).wait()
            total = total + part_got[h, last].astype(F32)
        return (total * scale).astype(BF16)

    early, late = list(range(PERIOD)), list(range(PERIOD, T))
    seq = [conv_state_ref[k].astype(F32) for k in range(3)]
    seq += [conv_ref[t].astype(F32) for t in early]
    bc_seq = [bc_state_ref[k, :, group_cols].astype(F32) for k in range(3)]
    bc_seq += [bc_ref[t, :, group_cols].astype(F32) for t in early]
    convolve(0, early, seq, bc_seq)
    contract(0, PERIOD)
    combine(
        0,
        early,
        lambda t: delta_ref[t].astype(F32),
        lambda t, cols: gate_ref[t, :, cols].astype(F32),
    )
    project(0)

    take_a, take_b = unpack_matrix(S, moved, R - 1, serve_take)
    own = 1.0 - named(S, R - 1, serve_take)
    own_rows = jnp.concatenate([own] * moved, axis=0)
    for o in range(R - 1):
        msg_copy(o).wait()
    arrived = got[...].reshape((R - 1) * 16, IL + GC + 128)
    new_gates[...] = dot(take_a, arrived[:, 0:IL]) + own_rows * gate_rows.astype(F32)
    new_conv = dot(take_b, arrived[:, 0:IL]) + own_rows * conv_rows.astype(F32)
    tail = dot(take_a, arrived[:, IL:])
    new_bc = tail[:, 0:GC] + own_rows * bc_rows.astype(F32)
    new_delta = tail[:, GC : GC + HL] + own_rows * delta_rows.astype(F32)
    seq = [conv_ref[t].astype(F32) if t < PERIOD else None for t in range(PERIOD)]
    seq = [None] * 3 + seq + [new_conv[k * S : (k + 1) * S] for k in range(moved)]
    bc_seq = [None] * 3 + [bc_ref[t, :, group_cols].astype(F32) for t in range(PERIOD)]
    bc_seq += [new_bc[k * S : (k + 1) * S] for k in range(moved)]
    convolve(1, late, seq, bc_seq)
    contract(1, moved)
    relay(0)
    combine(
        1,
        late,
        lambda t: new_delta[(t - PERIOD) * S : (t - PERIOD + 1) * S],
        lambda t, cols: new_gates[(t - PERIOD) * S : (t - PERIOD + 1) * S, cols],
    )
    project(1)

    out_ref[0:PERIOD] = finish_half(0, early).reshape(PERIOD, S, DL)
    half = DL // 2
    relay(1)
    give_a, give_b = pack_matrix(S, moved, R - 1, give_send)
    put_a, put_b = unpack_matrix(S, moved, R - 1, give_take)
    is_target = named(S, R - 1, give_take)
    keep_rows = jnp.concatenate([own * (1.0 - is_target)] * moved, axis=0)

    later = finish_half(1, late)
    packed = dot(give_a, later[:, 0:half]) + dot(give_b, later[:, half:])
    back[...] = packed.astype(BF16).reshape(R - 1, 16, half)

    def back_copy(o):
        return pltpu.make_async_remote_copy(
            src_ref=back.at[o],
            dst_ref=back_got.at[o],
            send_sem=back_send.at[o],
            recv_sem=back_recv.at[o],
            device_id={"rep": ahead(o)},
            device_id_type=MESH,
        )

    for o in range(R - 1):
        back_copy(o).start()
    stay = keep_rows * later.astype(F32)
    for o in range(R - 1):
        back_copy(o).wait()
    arrived = back_got[...].reshape((R - 1) * 16, half)
    left = (dot(put_a, arrived) + stay[:, 0:half]).astype(BF16)
    right = (dot(put_b, arrived) + stay[:, half:]).astype(BF16)
    out_ref[PERIOD:, :, 0:half] = left.reshape(moved, S, half)
    out_ref[PERIOD:, :, half:] = right.reshape(moved, S, half)


def body(R, TP, *arrays):
    (gate, conv, bc, delta, conv_w, conv_b, bc_w, bc_b, delta_b, decay, skip, gain, w, state,
     conv_state, bc_state, finish, plan) = arrays
    T, S, IL = gate.shape
    HL = delta.shape[2]
    NG = max(1, HL * GROUPS // HEADS)
    D = w.shape[1]
    DL = D // TP
    GC = NG * 2 * STATE
    wide = IL + GC + 128
    dims = (T, S, IL, HL, NG, R, TP, DL)
    vmem = pl.BlockSpec(memory_space=pltpu.VMEM)
    hbm = pl.BlockSpec(memory_space=pl.ANY)
    smem = pl.BlockSpec(memory_space=pltpu.SMEM)
    dma = pltpu.SemaphoreType.DMA
    half = DL // 2
    rows = PERIOD * S
    return pl.pallas_call(
        functools.partial(kernel, dims),
        out_shape=jax.ShapeDtypeStruct((T, S, DL), BF16),
        in_specs=[vmem] * 12 + [hbm, hbm] + [vmem] * 2 + [smem] * 2,
        out_specs=vmem,
        scratch_shapes=[
            pltpu.VMEM((S, HL, HEAD_DIM, STATE), F32),
            pltpu.VMEM((TP, IL, DL), BF16),
            pltpu.VMEM((R - 1, 16, wide), BF16),
            pltpu.VMEM((R - 1, 16, wide), BF16),
            pltpu.VMEM((T * S, IL), F32),
            pltpu.VMEM((T, S, NG * STATE), F32),
            pltpu.VMEM((2, 8, S, NG * STATE), F32),
            pltpu.VMEM((rows // S, S, IL), F32),
            pltpu.VMEM((rows, IL), F32),
            pltpu.VMEM((2, rows, IL), BF16),
            pltpu.VMEM((2, S, 128), F32),
            pltpu.VMEM((2, TP - 1, S, 128), F32),
            pltpu.VMEM((2, TP, rows, DL), F32),
            pltpu.VMEM((2, TP, rows, DL), BF16),
            pltpu.VMEM((2, TP, rows, DL), BF16),
            pltpu.VMEM((R - 1, 16, half), BF16),
            pltpu.VMEM((R - 1, 16, half), BF16),
            dma((S,)),
            dma((TP,)),
            dma((R - 1,)),
            dma((R - 1,)),
            dma((2, TP - 1)),
            dma((2, TP - 1)),
            dma((2, TP)),
            dma((2, TP)),
            dma((R - 1,)),
            dma((R - 1,)),
        ],
        compiler_params=pltpu.CompilerParams(
            collective_id=0, has_side_effects=True, vmem_limit_bytes=58 * 1024 * 1024
        ),
    )(
        gate,
        conv,
        bc,
        delta,
        conv_w,
        conv_b.reshape(1, -1),
        bc_w,
        bc_b.reshape(1, -1),
        delta_b.reshape(1, -1),
        decay.reshape(1, -1),
        skip.reshape(1, -1),
        gain.reshape(1, -1),
        w,
        state,
        conv_state.transpose(1, 0, 2),
        bc_state.transpose(1, 0, 2),
        finish,
        plan.transpose(0, 1, 3, 4, 2).reshape(R * CAP, 2, R),
    )


def solution(mesh):
    rows = ("parts", "rep")
    in_specs = (
        P(None, rows, "tp"),
        P(None, rows, "tp"),
        P(None, rows, None),
        P(None, rows, "tp"),
        P(None, "tp"),
        P("tp"),
        P(),
        P(),
        P("tp"),
        P("tp"),
        P("tp"),
        P("tp"),
        P("tp", None),
        P(rows, "tp", None, None),
        P(rows, None, "tp"),
        P(rows, None, None),
        P(rows),
        P("parts", None, None, None, None),
    )
    return jax.shard_map(
        functools.partial(body, mesh.shape["rep"], mesh.shape["tp"]),
        mesh=mesh,
        in_specs=in_specs,
        out_specs=P(None, rows, "tp"),
        check_vma=False,
    )
```
